256 devices in a mesh: ia: 8 (over z), ja: 4 (over y), ka: 8 (over x, core).
Axes of the slice: x: 4, y: 4, z: 8, core: 2. Of those that a mesh axis runs over, the one named last changes fastest.
Arguments:
- blocks: bfloat16 [8, 4, 16, 128, 128, 128], P('ia', 'ja', 'ka'), may hold values from -6 to 6
- coordinates: int32 [3, 8, 4, 16], P(None, 'ia', 'ja', 'ka'), may hold values from 0 to 3, as said below
- occupancy: int32 [8, 4, 16], P('ia', 'ja', 'ka'), may hold values from 0 to 1, as said below
- second_factor: bfloat16 [4, 512, 1024], P('ja', ('ia', 'ka')), may hold values from -12 to 12
- third_factor: bfloat16 [8, 512, 1024], P('ka', ('ia', 'ja')), may hold values from -0.0234375 to 0.0234375
- inverse_first: bfloat16 [1024, 1024], replicated
- inverse_second: bfloat16 [1024, 1024], replicated
Outputs:
- first_new: bfloat16 [8, 512, 1024], P('ia', ('ja', 'ka'))
- second_new: bfloat16 [4, 512, 1024], P('ja', ('ia', 'ka'))
The draws below stay inside these ranges and needn't reach their ends.
Inputs may be any that keep to these rules, and one draw needn't show every extreme that they name: `occupancy`: each device has two slots; its second slot is occupied only where its first is. A device with two blocks is followed along ka, cyclically, by a device with none. Some device holds two blocks. coordinates[0], [1], [2] of a slot are a block row among 4, a block row among 4 and a block layer among 4 of its device's ranges; the two slots of a device name different layers.
All inputs are finite; a program needn't handle non-finite values.
Results may differ from the reference program's by a relative error of at most 0.006.
Values may be sent and summed in bfloat16 or wider, within the bound.
No kernel may reach another device: no remote copies, remote signals or barrier semaphores. Data moves between devices by JAX's collectives and lax.ppermute only.
A program may use at most 128 MiB of HBM per device.

```python
import jax
import jax.numpy as jnp
from jax import lax

R = 1024
BLK = 128
SLOTS = 2
IB = 4
JB = 4
KB = 4
N_IA = 8
N_JA = 4
N_KA = 8


def draw_occupancy(key, part):
    subkeys = jax.random.split(jax.random.fold_in(key, 31), 3)
    cycles = N_IA * N_JA
    draws_raw = jax.random.randint(subkeys[0], (cycles, N_KA), 0, 20)
    counts = jnp.where(draws_raw < 7, 0, jnp.where(draws_raw < 14, 1, 2))
    forced_cycle = jax.random.randint(subkeys[1], (), 0, cycles)
    forced_place = jax.random.randint(subkeys[2], (), 0, N_KA)
    cycle_ids = jnp.arange(cycles)[:, None]
    positions = jnp.arange(N_KA)[None, :]
    counts = jnp.where((cycle_ids == forced_cycle) & (positions == forced_place), 2, counts)
    counts = jnp.where((cycle_ids == forced_cycle) & (positions == (forced_place + N_KA - 1) % N_KA), 0, counts)
    previous = jnp.roll(counts, 1, axis=1)
    counts = jnp.where(previous == 2, 0, counts)
    occupied = jnp.stack([counts >= 1, counts >= 2], axis=-1).astype(jnp.int32)
    return occupied.reshape(N_IA, N_JA, N_KA * SLOTS)


def draw_coordinates(key, part):
    subkeys = jax.random.split(jax.random.fold_in(key, 41), 4)
    shape_dev = (N_IA, N_JA, N_KA, SLOTS)
    first_rows = jax.random.randint(subkeys[0], shape_dev, 0, IB)
    second_rows = jax.random.randint(subkeys[1], shape_dev, 0, JB)
    layer_first = jax.random.randint(subkeys[2], (N_IA, N_JA, N_KA), 0, KB)
    layer_step = jax.random.randint(subkeys[3], (N_IA, N_JA, N_KA), 1, KB)
    layers = jnp.stack([layer_first, (layer_first + layer_step) % KB], axis=-1)
    stacked = jnp.stack([first_rows, second_rows, layers], axis=0)
    return stacked.reshape(3, N_IA, N_JA, N_KA * SLOTS).astype(jnp.int32)


def gram_inverse(noise, diag_key):
    diagonal = jax.random.uniform(diag_key, (R,), jnp.float32, 0.4, 1.0)
    symmetric = (noise + noise.T) * (0.2 / (2.0 * R) ** 0.5)
    on_diagonal = jnp.arange(R)[:, None] == jnp.arange(R)[None, :]
    return symmetric + jnp.where(on_diagonal, diagonal[None, :], 0.0)


def draw_inverse_first(key, part):
    subkeys = jax.random.split(jax.random.fold_in(key, 11), 2)
    noise = jax.random.normal(subkeys[0], (R, R), jnp.float32)
    return gram_inverse(noise, subkeys[1]).astype(jnp.bfloat16)


def draw_inverse_second(key, part):
    subkeys = jax.random.split(jax.random.fold_in(key, 12), 2)
    noise = jax.random.normal(subkeys[0], (R, R), jnp.float32)
    return gram_inverse(noise, subkeys[1]).astype(jnp.bfloat16)


def shard_levels(key, extent, pieces, least, largest):
    gain, own = 1.0, jax.random.fold_in(key, 6)
    for dim, shards_of in pieces:
        draws = jnp.exp(jax.random.uniform(jax.random.fold_in(own, dim), (shards_of,), jnp.float32, least / len(pieces), largest / len(pieces)))
        gain = gain * jnp.repeat(draws, extent[dim] // shards_of).reshape([-1 if axis == dim else 1 for axis in range(len(extent))])
    return gain


def gaussian(rng, extent, width, most, cuts=(), kind=jnp.bfloat16):
    drawn = width * jax.random.normal(rng, extent, jnp.float32)
    if cuts:
        drawn = drawn * shard_levels(rng, extent, cuts, -0.22, 0.18)
    return jnp.clip(drawn, -most, most).astype(kind)


def setup_inputs(seed: int = 0) -> dict:
    keys = jax.random.split(jax.random.key(seed), 8)
    return {
        "blocks": gaussian(keys[0], (N_IA, N_JA, N_KA * SLOTS, BLK, BLK, BLK), 1.0, 6.0, ((0, 8), (1, 4), (2, 8))),
        "coordinates": draw_coordinates(jax.random.fold_in(keys[7], 71), 0),
        "occupancy": draw_occupancy(jax.random.fold_in(keys[7], 71), 0),
        "second_factor": gaussian(keys[3], (N_JA, JB * BLK, R), 2.0, 12.0, ((0, 4), (1, 64))),
        "third_factor": gaussian(keys[4], (N_KA, KB * BLK, R), 0.004, 0.0234375, ((0, 8), (1, 32))),
        "inverse_first": draw_inverse_first(jax.random.fold_in(keys[7], 71), 0),
        "inverse_second": draw_inverse_second(jax.random.fold_in(keys[7], 71), 0),
    }


def reference(blocks, coordinates, occupancy, second_factor, third_factor, inverse_first, inverse_second):
    total_slots = N_IA * N_JA * N_KA * SLOTS
    flat_blocks = blocks.reshape(total_slots, BLK, BLK, BLK)
    places = coordinates.reshape(3, total_slots)
    occupied = occupancy.reshape(total_slots)
    slot_ids = jnp.arange(total_slots, dtype=jnp.int32)
    first_plane = slot_ids // (N_JA * N_KA * SLOTS)
    second_plane = (slot_ids // (N_KA * SLOTS)) % N_JA
    third_plane = (slot_ids // SLOTS) % N_KA
    row_block = (first_plane * IB + places[0]).astype(jnp.int32)
    col_block = (second_plane * JB + places[1]).astype(jnp.int32)
    layer_block = (third_plane * KB + places[2]).astype(jnp.int32)
    second_table = second_factor.reshape(N_JA * JB * BLK, R)
    third_table = third_factor.reshape(N_KA * KB * BLK, R)

    def mode_sum(target_rows, own_block, left_block, left_table, swapped):
        def add_block(totals, slot_index):
            def include(carry):
                tensor_block = lax.dynamic_index_in_dim(flat_blocks, slot_index, 0, keepdims=False)
                if swapped:
                    tensor_block = jnp.transpose(tensor_block, (1, 0, 2))
                left_slab = lax.dynamic_slice_in_dim(left_table, left_block[slot_index] * BLK, BLK, 0)
                layer_slab = lax.dynamic_slice_in_dim(third_table, layer_block[slot_index] * BLK, BLK, 0)
                khatri = (left_slab[:, None, :].astype(jnp.float32) * layer_slab[None, :, :].astype(jnp.float32)).astype(jnp.bfloat16)
                product = jnp.dot(tensor_block.reshape(BLK, BLK * BLK), khatri.reshape(BLK * BLK, R), preferred_element_type=jnp.float32)
                row_start = own_block[slot_index] * BLK
                current = lax.dynamic_slice_in_dim(carry, row_start, BLK, 0)
                return lax.dynamic_update_slice_in_dim(carry, current + product, row_start, 0)
            return lax.cond(occupied[slot_index] > 0, include, lambda carry: carry, totals), None
        zeroed = jnp.zeros((target_rows, R), jnp.float32)
        result, unused = lax.scan(add_block, zeroed, slot_ids)
        return result

    first_sum = mode_sum(N_IA * IB * BLK, row_block, col_block, second_table, False)
    first_new = jnp.dot(first_sum.astype(jnp.bfloat16), inverse_first, preferred_element_type=jnp.float32).astype(jnp.bfloat16)
    second_sum = mode_sum(N_JA * JB * BLK, col_block, row_block, first_new, True)
    second_new = jnp.dot(second_sum.astype(jnp.bfloat16), inverse_second, preferred_element_type=jnp.float32).astype(jnp.bfloat16)
    return first_new.reshape(N_IA, IB * BLK, R), second_new.reshape(N_JA, JB * BLK, R)
```

```python
import functools

import jax
import jax.numpy as jnp
from jax import lax
from jax.experimental import pallas as pl
from jax.experimental.pallas import tpu as pltpu
from jax.sharding import PartitionSpec as P

BLK = 128
CHUNK = 32
BF = jnp.bfloat16
F32 = jnp.float32


def rotated(x, axis, distance):
    n = lax.axis_size(axis)
    return lax.ppermute(x, axis, [(i, (i + distance) % n) for i in range(n)])


def core_swap(x):
    return lax.ppermute(x, "ka", [(i, i ^ 1) for i in range(lax.axis_size("ka"))])


def accumulate(x_ref, rows_ref, slab_ref, acc, slot, step):
    lhs = jnp.concatenate([x_ref[0, j] for j in range(CHUNK)], axis=1)
    groups = [rows_ref[step * (CHUNK // 8) + g] for g in range(CHUNK // 8)]
    width = acc.shape[-1] // 4
    for n in range(4):
        cols = slice(n * width, (n + 1) * width)
        slab = slab_ref[...].reshape(BLK, -1)[:, cols]
        khatri = jnp.concatenate(
            [slab * groups[j // 8][j % 8 : j % 8 + 1, cols] for j in range(CHUNK)], axis=0
        )
        part = jnp.dot(lhs, khatri, preferred_element_type=F32)

        @pl.when(step == 0)
        def _():
            acc[slot, :, cols] = part

        @pl.when(step > 0)
        def _():
            acc[slot, :, cols] += part


def first_kernel(
    sc, x_ref, own_ref, other_ref, c0, c1, c2, c3, out_ref, slabs_ref, rows, slab, acc
):
    slot, step = pl.program_id(0), pl.program_id(1)

    @pl.when(step == 0)
    def _():
        col, layer = sc[slot], sc[2 + slot]
        for e in range(4):
            for h in range(2):
                rows[h * 8 + sc[4 + e]] = own_ref[e, 2 * col + h]
                rows[h * 8 + sc[8 + e]] = other_ref[e, 2 * col + h]
        for e, piece in enumerate((c0, c1, c2, c3)):
            for g in range(2):
                slab[g * 4 + sc[12 + e]] = piece[2 * layer + g]
        slabs_ref[slot] = slab[...]

    accumulate(x_ref, rows, slab, acc, slot, step)

    @pl.when((slot == 1) & (step == pl.num_programs(1) - 1))
    def _():
        for b in range(4):
            for c in range(8):
                first = c * 16 + b * 4
                both = jnp.concatenate(
                    [acc[0, first : first + 4], acc[1, first : first + 4]], axis=0
                )
                out_ref[b * 8 + c] = both.astype(BF)


def second_kernel(x_ref, rows_ref, slabs_ref, out_ref, acc):
    slot, step = pl.program_id(0), pl.program_id(1)
    accumulate(x_ref, rows_ref.at[0], slabs_ref.at[0], acc, slot, step)

    @pl.when((slot == 1) & (step == pl.num_programs(1) - 1))
    def _():
        for c in range(8):
            parts = [
                acc[s, h * 64 + c * 8 : h * 64 + c * 8 + 8] for s in range(2) for h in range(2)
            ]
            out_ref[c] = jnp.concatenate(parts, axis=0).astype(BF)


PARAMS = pltpu.CompilerParams(vmem_limit_bytes=48 * 2**20)
COST = pl.CostEstimate(flops=2 * 2 * 128**3 * 1024, bytes_accessed=12 * 2**20, transcendentals=0)


def first_products(scalars, x, own, other, pieces):
    r = own.shape[-1]

    def whole(shape):
        return pl.BlockSpec(shape, lambda s, q, sc: (0,) * len(shape))

    return pl.pallas_call(
        first_kernel,
        grid_spec=pltpu.PrefetchScalarGridSpec(
            num_scalar_prefetch=1,
            grid=(2, BLK // CHUNK),
            in_specs=[
                pl.BlockSpec((1, CHUNK, BLK, BLK), lambda s, q, sc: (s, q, 0, 0)),
                whole(own.shape),
                whole(other.shape),
                *[whole(p.shape) for p in pieces],
            ],
            out_specs=[whole((32, 8, r)), whole((2, 8, 16, r))],
            scratch_shapes=[
                pltpu.VMEM((16, 8, r), BF),
                pltpu.VMEM((8, 16, r), BF),
                pltpu.VMEM((2, BLK, r), F32),
            ],
        ),
        out_shape=[
            jax.ShapeDtypeStruct((32, 8, r), BF),
            jax.ShapeDtypeStruct((2, 8, 16, r), BF),
        ],
        compiler_params=PARAMS,
        cost_estimate=COST,
    )(scalars, x, own, other, *pieces)


def second_products(x, rows, slabs):
    r = rows.shape[-1]
    return pl.pallas_call(
        second_kernel,
        grid=(2, BLK // CHUNK),
        in_specs=[
            pl.BlockSpec((1, CHUNK, BLK, BLK), lambda s, q: (s, q, 0, 0)),
            pl.BlockSpec((1, 16, 8, r), lambda s, q: (s, 0, 0, 0)),
            pl.BlockSpec((1, 8, 16, r), lambda s, q: (s, 0, 0, 0)),
        ],
        out_specs=pl.BlockSpec((8, 32, r), lambda s, q: (0, 0, 0)),
        out_shape=jax.ShapeDtypeStruct((8, 32, r), BF),
        scratch_shapes=[pltpu.VMEM((2, BLK, r), F32)],
        compiler_params=PARAMS,
        cost_estimate=COST,
    )(x, rows, slabs)


def plane_table(row, b, c):
    place = (jnp.arange(32) == b * 8 + c)[:, None]
    table = jnp.where(place, row[None, :], 0.0)
    table = table + core_swap(table)
    table = table + rotated(table, "ka", 2) + rotated(table, "ka", 4) + rotated(table, "ka", 6)
    return table + rotated(table, "ja", 1) + rotated(table, "ja", 2) + rotated(table, "ja", 3)


def body(
    blocks, coordinates, occupancy, second_factor, third_factor, inverse_first, inverse_second
):
    r = inverse_first.shape[0]
    b, c = lax.axis_index("ja"), lax.axis_index("ka")
    own_blocks = blocks.reshape(2, BLK, BLK, BLK)
    places = coordinates.reshape(3, 2)
    occupied = occupancy.reshape(2)

    mine = jnp.concatenate([second_factor[0], third_factor[0]], axis=0)
    along = lax.all_to_all(
        jnp.broadcast_to(mine, (8, *mine.shape)), "ia", 0, 0, tiled=True
    )
    layer_piece = along[:, 8:]
    row_piece = along[:, :8]
    pieces = [layer_piece] + [rotated(layer_piece, "ja", d) for d in (1, 3, 2)]
    own = jnp.stack([row_piece] + [rotated(row_piece, "ka", d) for d in (2, 6, 4)])
    other = core_swap(own)

    tag_row = jnp.concatenate(
        [places[0], places[1], occupied, jnp.zeros((122,), jnp.int32)]
    ).astype(F32)
    table = plane_table(tag_row, b, c)

    turns = jnp.array([0, 2, 6, 4], jnp.int32)
    scalars = jnp.concatenate(
        [
            places[1],
            places[2],
            (c - turns) % 8,
            ((c ^ 1) - turns) % 8,
            (b - jnp.array([0, 1, 3, 2], jnp.int32)) % 4,
        ]
    ).astype(jnp.int32)
    turned = jnp.transpose(own_blocks, (0, 2, 1, 3))
    contribution, slabs = first_products(scalars, turned, own, other, pieces)

    arrived = lax.all_to_all(contribution, ("ja", "ka"), 0, 0, tiled=True)
    tag = jnp.repeat(table[:, 0:2].reshape(64), 4)
    weight = jnp.repeat(table[:, 4:6].reshape(64), 4)
    fine = jnp.arange(256) % 4
    owned_block, owned_fine = jnp.arange(16) // 4, jnp.arange(16) % 4
    match = (owned_block[:, None] == tag[None, :]) & (owned_fine[:, None] == fine[None, :])
    pick = jnp.where(match & (weight[None, :] > 0), 1, 0).astype(BF)
    give = jnp.where(match.T, 1, 0).astype(BF)
    owned = jnp.dot(pick, arrived.reshape(256, r), preferred_element_type=F32)
    new_rows = jnp.dot(owned.astype(BF), inverse_first, preferred_element_type=F32).astype(BF)
    sent = jnp.dot(give, new_rows, preferred_element_type=F32).astype(BF).reshape(32, 8, r)
    got = lax.all_to_all(sent, ("ja", "ka"), 0, 0, tiled=True)
    rows = got.reshape(4, 8, 2, 4, r).transpose(2, 1, 0, 3, 4).reshape(2, 16, 8, r)

    by_block = new_rows.reshape(4, 4, r)
    first_new = jnp.zeros((4, 4, r), BF)
    for d in range(4):
        piece = lax.dynamic_index_in_dim(by_block, (b + d) % 4, 0)
        if d:
            piece = rotated(piece, "ja", d)
        first_new = lax.dynamic_update_slice_in_dim(first_new, piece, (b - d) % 4, 0)
    first_new = first_new.reshape(1, 16, r)

    contribution = second_products(own_blocks, rows, slabs)
    arrived = lax.all_to_all(contribution, "ka", 0, 0, tiled=True)
    mine = lax.dynamic_slice_in_dim(table, b * 8, 8, 0)
    tag = jnp.repeat(mine[:, 2:4].reshape(16), 16)
    weight = jnp.repeat(mine[:, 4:6].reshape(16), 16)
    fine = jnp.arange(256) % 16
    owned_block, owned_fine = jnp.arange(64) // 16, jnp.arange(64) % 16
    match = (owned_block[:, None] == tag[None, :]) & (owned_fine[:, None] == fine[None, :])
    pick = jnp.where(match & (weight[None, :] > 0), 1, 0).astype(BF)
    partial = jnp.dot(pick, arrived.reshape(256, r), preferred_element_type=F32).astype(BF)
    last = lax.all_to_all(partial.reshape(8, 8, r), "ia", 0, 0, tiled=True)
    owned = jnp.sum(last.astype(F32), axis=0)
    second_new = jnp.dot(owned.astype(BF), inverse_second, preferred_element_type=F32)
    return first_new, second_new.astype(BF)[None]


def solution(mesh):
    in_specs = (
        P("ia", "ja", "ka", None, None, None),
        P(None, "ia", "ja", "ka"),
        P("ia", "ja", "ka"),
        P("ja", ("ia", "ka"), None),
        P("ka", ("ia", "ja"), None),
        P(),
        P(),
    )
    out_specs = (P("ia", ("ja", "ka"), None), P("ja", ("ia", "ka"), None))
    return jax.shard_map(body, mesh=mesh, in_specs=in_specs, out_specs=out_specs, check_vma=False)
```

```python
import jax
import jax.numpy as jnp
from jax import lax
from jax.experimental import pallas as pl
from jax.experimental.pallas import tpu as pltpu
from jax.sharding import PartitionSpec as P

BLK = 128
CHUNK = 64
BF = jnp.bfloat16
F32 = jnp.float32


def rotated(x, axis, distance):
    n = lax.axis_size(axis)
    return lax.ppermute(x, axis, [(i, (i + distance) % n) for i in range(n)])


def core_swap(x):
    return lax.ppermute(x, "ka", [(i, i ^ 1) for i in range(lax.axis_size("ka"))])


def products(planes, group, rows, slab, acc, step):
    @pl.when(step == 0)
    def _():
        acc[...] = jnp.zeros_like(acc)

    left = rows[pl.ds(pl.multiple_of(step * CHUNK, CHUNK), CHUNK), :].astype(BF)
    width = acc.shape[-1] // 4
    for first in range(0, CHUNK, group):
        tiles = planes(first)
        lhs = jnp.concatenate([tiles[j] for j in range(group)], axis=1)
        for n in range(4):
            cols = slice(n * width, (n + 1) * width)
            layer = slab[:, cols]
            khatri = jnp.concatenate(
                [layer * left[j : j + 1, cols] for j in range(first, first + group)], axis=0
            )
            acc[:, cols] += jnp.dot(lhs, khatri, preferred_element_type=F32)


def for_slot(slot, when, todo):
    for s in range(2):

        @pl.when((slot == s) & when)
        def _():
            todo(s)


def take_layers(place, layer_refs, slab):
    def todo(s):
        for ref, distance in zip(layer_refs, (0, 1, 3, 2)):
            owner = lax.rem(place - distance + 4, 4)
            for g in range(2):
                first = pl.multiple_of((g * 4 + owner) * 16, 16)
                slab[pl.ds(first, 16), :] = ref[s * 2 + g]

    return todo


def first_kernel(sc, x_ref, own_ref, other_ref, l0, l1, l2, l3, out_ref, rows, slab, acc):
    slot, step = pl.program_id(0), pl.program_id(1)
    for_slot(slot, step == 0, take_layers(sc[10], (l0, l1, l2, l3), slab))

    @pl.when(step == 0)
    def _():
        col = sc[slot]
        for e in range(4):
            for h in range(2):
                for ref, owner in ((own_ref, sc[2 + e]), (other_ref, sc[6 + e])):
                    first = pl.multiple_of((h * 8 + owner) * 8, 8)
                    rows[pl.ds(first, 8), :] = ref[e, 2 * col + h].astype(F32)

    def planes(first):
        return jnp.swapaxes(x_ref[0, :, first : first + 16, :], 0, 1)

    products(planes, 16, rows, slab, acc, step)

    def write(s):
        for b in range(4):
            for c in range(8):
                first = c * 16 + b * 4
                out_ref[b * 8 + c, s * 4 : s * 4 + 4] = acc[first : first + 4].astype(BF)

    for_slot(slot, step == pl.num_programs(1) - 1, write)


def second_kernel(
    sc, x_ref, got_ref, l0, l1, l2, l3, inverse_ref, out_ref, rows, slab, acc, done
):
    slot, step = pl.program_id(0), pl.program_id(1)
    for_slot(slot, step == 0, take_layers(sc[10], (l0, l1, l2, l3), slab))

    def take_rows(s):
        for c in range(8):
            for b in range(4):
                first = c * 16 + b * 4
                rows[first : first + 4] = got_ref[b * 8 + c, s * 4 : s * 4 + 4].astype(F32)

    for_slot(slot, step == 0, take_rows)
    products(lambda first: x_ref[0, first : first + 32], 32, rows, slab, acc, step)

    def write(s):
        done[s * BLK : (s + 1) * BLK] = acc[...].astype(BF)
        if s == 0:
            return
        turned = jnp.dot(done[...], inverse_ref[...], preferred_element_type=F32).astype(BF)
        for t in range(2):
            for c in range(8):
                for h in range(2):
                    first, to = t * BLK + h * 64 + c * 8, t * 16 + h * 8
                    out_ref[c, to : to + 8] = turned[first : first + 8]

    for_slot(slot, step == pl.num_programs(1) - 1, write)


PARAMS = pltpu.CompilerParams(vmem_limit_bytes=57 * 2**20)
COST = pl.CostEstimate(flops=2 * 2 * 128**3 * 1024, bytes_accessed=12 * 2**20, transcendentals=0)


def whole(x):
    return pl.BlockSpec(x.shape, lambda *ids: (0,) * len(x.shape))


def slot_products(kernel, scalars, x, by_column, others, out_shape, scratch=()):
    r = out_shape[-1]
    if by_column:
        x_spec = pl.BlockSpec((1, BLK, CHUNK, BLK), lambda s, q, *sc: (s, 0, q, 0))
    else:
        x_spec = pl.BlockSpec((1, CHUNK, BLK, BLK), lambda s, q, *sc: (s, q, 0, 0))
    return pl.pallas_call(
        kernel,
        grid_spec=pltpu.PrefetchScalarGridSpec(
            num_scalar_prefetch=len(scalars),
            grid=(2, BLK // CHUNK),
            in_specs=[x_spec, *[whole(o) for o in others]],
            out_specs=whole(jax.ShapeDtypeStruct(out_shape, BF)),
            scratch_shapes=[
                pltpu.VMEM((BLK, r), F32),
                pltpu.VMEM((BLK, r), BF),
                pltpu.VMEM((BLK, r), F32),
                *scratch,
            ],
        ),
        out_shape=jax.ShapeDtypeStruct(out_shape, BF),
        compiler_params=PARAMS,
        cost_estimate=COST,
    )(*scalars, x, *others)


def choose_kernel(sc, along_ref, *refs):
    *send_refs, rows_ref = refs
    for ref, distance in zip(send_refs, (0, 1, 3, 2)):
        to = lax.rem(sc[8] + distance, 4)
        for s in range(2):
            for g in range(2):
                ref[s * 2 + g] = along_ref[2 * sc[to * 2 + s] + g, 0:16]
    for a in range(8):
        rows_ref[a] = along_ref[a, 16:24]


def chosen_pieces(layers, along):
    r = along.shape[-1]
    outs = [jax.ShapeDtypeStruct((4, 16, r), BF)] * 4 + [jax.ShapeDtypeStruct((8, 8, r), BF)]
    return pl.pallas_call(
        choose_kernel,
        grid_spec=pltpu.PrefetchScalarGridSpec(
            num_scalar_prefetch=1,
            grid=(1,),
            in_specs=[whole(along)],
            out_specs=[whole(o) for o in outs],
        ),
        out_shape=outs,
        compiler_params=pltpu.CompilerParams(vmem_limit_bytes=16 * 2**20),
    )(layers, along)


def body(
    blocks, coordinates, occupancy, second_factor, third_factor, inverse_first, inverse_second
):
    r = inverse_first.shape[0]
    b, c = lax.axis_index("ja"), lax.axis_index("ka")
    own_blocks = blocks.reshape(2, BLK, BLK, BLK)
    places = coordinates.reshape(3, 2)

    mine = jnp.concatenate([third_factor[0], second_factor[0]], axis=0)
    along = lax.all_to_all(
        jnp.broadcast_to(mine, (8, *mine.shape)), "ia", 0, 0, tiled=True
    )
    tags = jnp.concatenate(
        [places.reshape(6), occupancy.reshape(2), jnp.zeros((120,), jnp.int32)]
    ).astype(F32)
    column = jnp.where((jnp.arange(4) == b)[:, None], tags[None, :], 0.0)
    column = column + rotated(column, "ja", 1) + rotated(column, "ja", 2) + rotated(column, "ja", 3)
    along, column = lax.optimization_barrier((along, column))

    layers = jnp.concatenate([column[:, 4:6].reshape(8), b[None]]).astype(jnp.int32)
    *send, row_piece = chosen_pieces(layers, along)
    slabs = [send[0]] + [rotated(send[e], "ja", d) for e, d in ((1, 1), (2, 3), (3, 2))]
    own = [row_piece] + [rotated(row_piece, "ka", d) for d in (2, 6, 4)]
    own, slabs = lax.optimization_barrier((own, slabs))
    own = jnp.stack(own)
    other = core_swap(own)

    turns = jnp.array([0, 2, 6, 4], jnp.int32)
    scalars = jnp.concatenate([places[1], (c - turns) % 8, ((c ^ 1) - turns) % 8, b[None]])
    scalars = scalars.astype(jnp.int32)
    contribution = slot_products(
        first_kernel,
        (scalars,),
        own_blocks,
        True,
        (own, other, *slabs),
        (32, 8, r),
    )

    arrived = lax.all_to_all(contribution, ("ja", "ka"), 0, 0, tiled=True)
    contribution, column = lax.optimization_barrier((contribution, column))
    table = jnp.where((jnp.arange(8) == c)[None, :, None], column[:, None, :], 0.0)
    table = table.reshape(32, 128)
    table = table + core_swap(table)
    table = table + rotated(table, "ka", 2) + rotated(table, "ka", 4) + rotated(table, "ka", 6)
    tag = jnp.repeat(table[:, 0:2].reshape(64), 4)
    weight = jnp.repeat(table[:, 6:8].reshape(64), 4)
    fine = jnp.arange(256) % 4
    owned_block, owned_fine = jnp.arange(16) // 4, jnp.arange(16) % 4
    match = (owned_block[:, None] == tag[None, :]) & (owned_fine[:, None] == fine[None, :])
    pick = jnp.where(match & (weight[None, :] > 0), 1, 0).astype(BF)
    give = jnp.where(match.T, 1, 0).astype(BF)
    owned = jnp.dot(pick, arrived.reshape(256, r), preferred_element_type=F32)
    new_rows = jnp.dot(owned.astype(BF), inverse_first, preferred_element_type=F32).astype(BF)
    sent = jnp.dot(give, new_rows, preferred_element_type=F32).astype(BF).reshape(32, 8, r)
    got = lax.all_to_all(sent, ("ja", "ka"), 0, 0, tiled=True)

    by_block = new_rows.reshape(4, 4, r)
    first_new = jnp.zeros((4, 4, r), BF)
    for d in range(4):
        piece = lax.dynamic_index_in_dim(by_block, (b + d) % 4, 0)
        if d:
            piece = rotated(piece, "ja", d)
        first_new = lax.dynamic_update_slice_in_dim(first_new, piece, (b - d) % 4, 0)
    first_new = first_new.reshape(1, 16, r)

    contribution = slot_products(
        second_kernel,
        (scalars,),
        own_blocks,
        False,
        (got, *slabs, inverse_second),
        (8, 32, r),
        (pltpu.VMEM((2 * BLK, r), BF),),
    )
    arrived = lax.all_to_all(contribution, "ka", 0, 0, tiled=True)
    mine = lax.dynamic_slice_in_dim(table, b * 8, 8, 0)
    tag = jnp.repeat(mine[:, 2:4].reshape(16), 16)
    weight = jnp.repeat(mine[:, 6:8].reshape(16), 16)
    fine = jnp.arange(256) % 16
    owned_block, owned_fine = jnp.arange(64) // 16, jnp.arange(64) % 16
    match = (owned_block[:, None] == tag[None, :]) & (owned_fine[:, None] == fine[None, :])
    pick = jnp.where(match & (weight[None, :] > 0), 1, 0).astype(BF)
    partial = jnp.dot(pick, arrived.reshape(256, r), preferred_element_type=F32).astype(BF)
    last = lax.all_to_all(partial.reshape(8, 8, r), "ia", 0, 0, tiled=True)
    total = last[0].astype(F32)
    for a in range(1, 8):
        total = total + last[a].astype(F32)
    return first_new, total.astype(BF)[None]


def solution(mesh):
    in_specs = (
        P("ia", "ja", "ka", None, None, None),
        P(None, "ia", "ja", "ka"),
        P("ia", "ja", "ka"),
        P("ja", ("ia", "ka"), None),
        P("ka", ("ia", "ja"), None),
        P(),
        P(),
    )
    out_specs = (P("ia", ("ja", "ka"), None), P("ja", ("ia", "ka"), None))
    return jax.shard_map(body, mesh=mesh, in_specs=in_specs, out_specs=out_specs, check_vma=False)
```

```python
import jax
import jax.numpy as jnp
from jax import lax
from jax.experimental import pallas as pl
from jax.experimental.pallas import tpu as pltpu
from jax.sharding import PartitionSpec as P

BLK = 128
CHUNK = 32
BF = jnp.bfloat16
F32 = jnp.float32


def rotated(x, axis, distance):
    n = lax.axis_size(axis)
    return lax.ppermute(x, axis, [(i, (i + distance) % n) for i in range(n)])


def core_swap(x):
    return lax.ppermute(x, "ka", [(i, i ^ 1) for i in range(lax.axis_size("ka"))])


def products(planes, group, rows, slab, acc, step):
    @pl.when(step == 0)
    def _():
        acc[...] = jnp.zeros_like(acc)

    left = rows[pl.ds(pl.multiple_of(step * CHUNK, CHUNK), CHUNK), :].astype(BF)
    width = acc.shape[-1] // 4
    for first in range(0, CHUNK, group):
        tiles = planes(first)
        lhs = jnp.concatenate([tiles[j] for j in range(group)], axis=1)
        for n in range(4):
            cols = slice(n * width, (n + 1) * width)
            layer = slab[:, cols]
            khatri = jnp.concatenate(
                [layer * left[j : j + 1, cols] for j in range(first, first + group)], axis=0
            )
            acc[:, cols] += jnp.dot(lhs, khatri, preferred_element_type=F32)


def for_slot(slot, when, todo):
    for s in range(2):

        @pl.when((slot == s) & when)
        def _():
            todo(s)


def take_layers(layer_refs, slab):
    def todo(s):
        for ref, distance in zip(layer_refs, (0, 1, 3, 2)):
            owner = lax.rem(lax.axis_index("ja") - distance + 4, 4)
            for g in range(2):
                first = pl.multiple_of((g * 4 + owner) * 16, 16)
                slab[pl.ds(first, 16), :] = ref[s * 2 + g]

    return todo


def first_kernel(
    sc, x_ref, own_ref, other_ref, l0, l1, l2, l3, tags_ref, out_ref, table_ref, rows, slab, acc
):
    slot, step = pl.program_id(0), pl.program_id(1)
    for_slot(slot, step == 0, take_layers((l0, l1, l2, l3), slab))

    @pl.when(step == 0)
    def _():
        col, c = sc[2 + slot], lax.axis_index("ka")
        for e, turn in enumerate((0, 2, 6, 4)):
            mine = lax.rem(c - turn + 8, 8)
            theirs = mine + 1 - 2 * lax.rem(c, 2)
            for h in range(2):
                for ref, owner in ((own_ref, mine), (other_ref, theirs)):
                    first = pl.multiple_of((h * 8 + owner) * 8, 8)
                    rows[pl.ds(first, 8), :] = ref[e, 2 * col + h].astype(F32)

    @pl.when((slot == 0) & (step == 0))
    def _():
        table_ref[...] = jnp.zeros_like(table_ref)
        for b in range(4):
            table_ref[pl.ds(b * 8 + lax.axis_index("ka"), 1), :] = tags_ref[b : b + 1, :]

    def planes(first):
        return jnp.swapaxes(x_ref[0, :, first : first + 16, :], 0, 1)

    products(planes, 16, rows, slab, acc, step)

    def write(s):
        for b in range(4):
            for c in range(8):
                first = c * 16 + b * 4
                out_ref[b * 8 + c, s * 4 : s * 4 + 4] = acc[first : first + 4].astype(BF)

    for_slot(slot, step == pl.num_programs(1) - 1, write)


def second_kernel(
    x_hbm, inverse_hbm, got_ref, l0, l1, l2, l3, out_ref, rows, slab, acc, done, *fetched
):
    x_ref, inverse_ref, x_sems, inverse_sem = fetched

    def fetch(slot, step):
        part = pl.ds(pl.multiple_of(step * CHUNK, CHUNK), CHUNK)
        return pltpu.make_async_copy(
            x_hbm.at[slot, part], x_ref.at[slot, part], x_sems.at[slot, step]
        )

    for slot in range(2):
        for step in range(BLK // CHUNK):
            fetch(slot, step).start()
    inverse_copy = pltpu.make_async_copy(inverse_hbm, inverse_ref, inverse_sem)
    inverse_copy.start()
    for slot in range(2):
        take_layers((l0, l1, l2, l3), slab)(slot)
        for c in range(8):
            for b in range(4):
                first = c * 16 + b * 4
                rows[first : first + 4] = got_ref[b * 8 + c, slot * 4 : slot * 4 + 4].astype(F32)

        @pl.loop(0, BLK // CHUNK)
        def _(step):
            fetch(slot, step).wait()
            base = pl.multiple_of(step * CHUNK, CHUNK)
            products(
                lambda first: x_ref[slot, pl.ds(base + first, 32)], 32, rows, slab, acc, step
            )

        done[slot * BLK : (slot + 1) * BLK] = acc[...].astype(BF)
    inverse_copy.wait()
    turned = jnp.dot(done[...], inverse_ref[...], preferred_element_type=F32).astype(BF)
    for slot in range(2):
        for c in range(8):
            for h in range(2):
                first, to = slot * BLK + h * 64 + c * 8, slot * 16 + h * 8
                out_ref[c, to : to + 8] = turned[first : first + 8]


PARAMS = pltpu.CompilerParams(vmem_limit_bytes=51 * 2**20)
COST = pl.CostEstimate(flops=2 * 2 * 128**3 * 1024, bytes_accessed=12 * 2**20, transcendentals=0)


def whole(x):
    return pl.BlockSpec(x.shape, lambda *ids: (0,) * len(x.shape))


def scratch_for(r):
    return [pltpu.VMEM((BLK, r), F32), pltpu.VMEM((BLK, r), BF), pltpu.VMEM((BLK, r), F32)]


def first_products(scalars, x, others):
    r = others[0].shape[-1]
    outs = [jax.ShapeDtypeStruct((32, 8, r), BF), jax.ShapeDtypeStruct((32, 128), F32)]
    return pl.pallas_call(
        first_kernel,
        grid_spec=pltpu.PrefetchScalarGridSpec(
            num_scalar_prefetch=1,
            grid=(2, BLK // CHUNK),
            in_specs=[
                pl.BlockSpec((1, BLK, CHUNK, BLK), lambda s, q, sc: (s, 0, q, 0)),
                *[whole(o) for o in others],
            ],
            out_specs=[whole(o) for o in outs],
            scratch_shapes=scratch_for(r),
        ),
        out_shape=outs,
        compiler_params=PARAMS,
        cost_estimate=COST,
    )(scalars, x, *others)


def second_products(x, inverse, others):
    r = inverse.shape[0]
    out = jax.ShapeDtypeStruct((8, 32, r), BF)
    return pl.pallas_call(
        second_kernel,
        grid=(1,),
        in_specs=[
            *[pl.BlockSpec(memory_space=pltpu.HBM)] * 2,
            *[whole(o) for o in others],
        ],
        out_specs=whole(out),
        scratch_shapes=[
            *scratch_for(r),
            pltpu.VMEM((2 * BLK, r), BF),
            pltpu.VMEM(x.shape, BF),
            pltpu.VMEM((r, r), BF),
            pltpu.SemaphoreType.DMA((2, BLK // CHUNK)),
            pltpu.SemaphoreType.DMA(()),
        ],
        out_shape=out,
        compiler_params=PARAMS,
        cost_estimate=COST,
    )(x, inverse, *others)


def choose_kernel(sc, along_ref, *refs):
    *send_refs, rows_ref = refs
    for ref, distance in zip(send_refs, (0, 1, 3, 2)):
        to = lax.rem(lax.axis_index("ja") + distance, 4)
        for s in range(2):
            for g in range(2):
                ref[s * 2 + g] = along_ref[2 * sc[to * 2 + s] + g, 0:16]
    for a in range(8):
        rows_ref[a] = along_ref[a, 16:24]


def chosen_pieces(layers, along):
    r = along.shape[-1]
    outs = [jax.ShapeDtypeStruct((4, 16, r), BF)] * 4 + [jax.ShapeDtypeStruct((8, 8, r), BF)]
    return pl.pallas_call(
        choose_kernel,
        grid_spec=pltpu.PrefetchScalarGridSpec(
            num_scalar_prefetch=1,
            grid=(1,),
            in_specs=[whole(along)],
            out_specs=[whole(o) for o in outs],
        ),
        out_shape=outs,
        compiler_params=pltpu.CompilerParams(vmem_limit_bytes=16 * 2**20),
    )(layers, along)


def body(
    blocks, coordinates, occupancy, second_factor, third_factor, inverse_first, inverse_second
):
    r = inverse_first.shape[0]
    b, c = lax.axis_index("ja"), lax.axis_index("ka")
    own_blocks = blocks.reshape(2, BLK, BLK, BLK)
    places = coordinates.reshape(3, 2)

    mine = jnp.concatenate([third_factor[0], second_factor[0]], axis=0)
    along = lax.all_to_all(
        jnp.broadcast_to(mine, (8, *mine.shape)), "ia", 0, 0, tiled=True
    )
    tags = jnp.concatenate(
        [places.reshape(6), occupancy.reshape(2), jnp.zeros((120,), jnp.int32)]
    ).astype(F32)
    column = jnp.where((jnp.arange(4) == b)[:, None], tags[None, :], 0.0)
    column = column + rotated(column, "ja", 1) + rotated(column, "ja", 2) + rotated(column, "ja", 3)
    along, column = lax.optimization_barrier((along, column))

    layers = column[:, 4:6].reshape(8).astype(jnp.int32)
    *send, row_piece = chosen_pieces(layers, along)
    slabs = [send[0]] + [rotated(send[e], "ja", d) for e, d in ((1, 1), (2, 3), (3, 2))]
    own = [row_piece] + [rotated(row_piece, "ka", d) for d in (2, 6, 4)]
    own, slabs = lax.optimization_barrier((own, slabs))
    own = jnp.stack(own)
    other = core_swap(own)

    contribution, table = first_products(
        places.reshape(6), own_blocks, (own, other, *slabs, column)
    )

    arrived = lax.all_to_all(contribution, ("ja", "ka"), 0, 0, tiled=True)
    table = table + core_swap(table)
    table = table + rotated(table, "ka", 2) + rotated(table, "ka", 4) + rotated(table, "ka", 6)
    tag = jnp.repeat(table[:, 0:2].reshape(64), 4)
    weight = jnp.repeat(table[:, 6:8].reshape(64), 4)
    fine = jnp.arange(256) % 4
    owned_block, owned_fine = jnp.arange(16) // 4, jnp.arange(16) % 4
    match = (owned_block[:, None] == tag[None, :]) & (owned_fine[:, None] == fine[None, :])
    pick = jnp.where(match & (weight[None, :] > 0), 1, 0).astype(BF)
    give = jnp.where(match.T, 1, 0).astype(BF)
    owned = jnp.dot(pick, arrived.reshape(256, r), preferred_element_type=F32)
    new_rows = jnp.dot(owned.astype(BF), inverse_first, preferred_element_type=F32).astype(BF)
    sent = jnp.dot(give, new_rows, preferred_element_type=F32).astype(BF).reshape(32, 8, r)
    got = lax.all_to_all(sent, ("ja", "ka"), 0, 0, tiled=True)

    by_block = new_rows.reshape(4, 4, r)
    first_new = jnp.zeros((4, 4, r), BF)
    for d in range(4):
        piece = lax.dynamic_index_in_dim(by_block, (b + d) % 4, 0)
        if d:
            piece = rotated(piece, "ja", d)
        first_new = lax.dynamic_update_slice_in_dim(first_new, piece, (b - d) % 4, 0)
    first_new = first_new.reshape(1, 16, r)

    contribution = second_products(own_blocks, inverse_second, (got, *slabs))
    arrived = lax.all_to_all(contribution, "ka", 0, 0, tiled=True)
    mine = lax.dynamic_slice_in_dim(table, b * 8, 8, 0)
    tag = jnp.repeat(mine[:, 2:4].reshape(16), 16)
    weight = jnp.repeat(mine[:, 6:8].reshape(16), 16)
    fine = jnp.arange(256) % 16
    owned_block, owned_fine = jnp.arange(64) // 16, jnp.arange(64) % 16
    match = (owned_block[:, None] == tag[None, :]) & (owned_fine[:, None] == fine[None, :])
    pick = jnp.where(match & (weight[None, :] > 0), 1, 0).astype(BF)
    partial = jnp.dot(pick, arrived.reshape(256, r), preferred_element_type=F32).astype(BF)
    last = lax.all_to_all(partial.reshape(8, 8, r), "ia", 0, 0, tiled=True)
    total = last[0].astype(F32)
    for a in range(1, 8):
        total = total + last[a].astype(F32)
    return first_new, total.astype(BF)[None]


def solution(mesh):
    in_specs = (
        P("ia", "ja", "ka", None, None, None),
        P(None, "ia", "ja", "ka"),
        P("ia", "ja", "ka"),
        P("ja", ("ia", "ka"), None),
        P("ka", ("ia", "ja"), None),
        P(),
        P(),
    )
    out_specs = (P("ia", ("ja", "ka"), None), P("ja", ("ia", "ka"), None))
    return jax.shard_map(body, mesh=mesh, in_specs=in_specs, out_specs=out_specs, check_vma=False)
```

```python
import jax
import jax.numpy as jnp
from jax import lax
from jax.experimental import pallas as pl
from jax.experimental.pallas import tpu as pltpu
from jax.sharding import PartitionSpec as P

BLK = 128
CHUNK = 32
BF = jnp.bfloat16
F32 = jnp.float32


def rotated(x, axis, distance):
    n = lax.axis_size(axis)
    return lax.ppermute(x, axis, [(i, (i + distance) % n) for i in range(n)])


def core_swap(x):
    return lax.ppermute(x, "ka", [(i, i ^ 1) for i in range(lax.axis_size("ka"))])


def products(planes, group, rows, slab, acc, step):
    @pl.when(step == 0)
    def _():
        acc[...] = jnp.zeros_like(acc)

    left = rows[pl.ds(pl.multiple_of(step * CHUNK, CHUNK), CHUNK), :].astype(BF)
    width = acc.shape[-1] // 4
    for first in range(0, CHUNK, group):
        tiles = planes(first)
        lhs = jnp.concatenate([tiles[j] for j in range(group)], axis=1)
        for n in range(4):
            cols = slice(n * width, (n + 1) * width)
            layer = slab[:, cols]
            khatri = jnp.concatenate(
                [layer * left[j : j + 1, cols] for j in range(first, first + group)], axis=0
            )
            acc[:, cols] += jnp.dot(lhs, khatri, preferred_element_type=F32)


def for_slot(slot, when, todo):
    for s in range(2):

        @pl.when((slot == s) & when)
        def _():
            todo(s)


def layers_kernel(l0, l1, l2, l3, out_ref):
    for ref, distance in zip((l0, l1, l2, l3), (0, 1, 3, 2)):
        owner = lax.rem(lax.axis_index("ja") - distance + 4, 4)
        for s in range(2):
            for g in range(2):
                first = pl.multiple_of((g * 4 + owner) * 16, 16)
                out_ref[s, pl.ds(first, 16), :] = ref[s * 2 + g]


def layer_slabs(pieces):
    out = jax.ShapeDtypeStruct((2, BLK, pieces[0].shape[-1]), BF)
    return pl.pallas_call(
        layers_kernel,
        grid=(1,),
        in_specs=[pl.BlockSpec(memory_space=pltpu.VMEM)] * 4,
        out_specs=whole(out),
        out_shape=out,
        compiler_params=PARAMS,
        cost_estimate=pl.CostEstimate(
            flops=2 * 128**3 * 4096, bytes_accessed=2**20, transcendentals=0
        ),
    )(*pieces)


def first_kernel(
    sc, x_ref, own_ref, other_ref, tags_ref, slab_ref, out_ref, table_ref, rows, acc
):
    slot, step = pl.program_id(0), pl.program_id(1)

    @pl.when(step == 0)
    def _():
        col, c = sc[2 + slot], lax.axis_index("ka")
        for e, turn in enumerate((0, 2, 6, 4)):
            mine = lax.rem(c - turn + 8, 8)
            theirs = mine + 1 - 2 * lax.rem(c, 2)
            for h in range(2):
                for ref, owner in ((own_ref, mine), (other_ref, theirs)):
                    first = pl.multiple_of((h * 8 + owner) * 8, 8)
                    rows[pl.ds(first, 8), :] = ref[e, 2 * col + h].astype(F32)

    @pl.when((slot == 0) & (step == 0))
    def _():
        table_ref[...] = jnp.zeros_like(table_ref)
        for b in range(4):
            table_ref[pl.ds(b * 8 + lax.axis_index("ka"), 1), :] = tags_ref[b : b + 1, :]

    def planes(first):
        return jnp.swapaxes(x_ref[0, :, first : first + 16, :], 0, 1)

    products(planes, 16, rows, slab_ref.at[0], acc, step)

    def write(s):
        for b in range(4):
            for c in range(8):
                first = c * 16 + b * 4
                out_ref[b * 8 + c, s * 4 : s * 4 + 4] = acc[first : first + 4].astype(BF)

    for_slot(slot, step == pl.num_programs(1) - 1, write)


def second_kernel(
    x_hbm, inverse_hbm, got_ref, slabs_ref, out_ref, rows, acc, done, *fetched
):
    x_ref, inverse_ref, x_sems, inverse_sem = fetched

    def fetch(slot, step):
        part = pl.ds(pl.multiple_of(step * CHUNK, CHUNK), CHUNK)
        return pltpu.make_async_copy(
            x_hbm.at[slot, part], x_ref.at[slot, part], x_sems.at[slot, step]
        )

    for slot in range(2):
        for step in range(BLK // CHUNK):
            fetch(slot, step).start()
    inverse_copy = pltpu.make_async_copy(inverse_hbm, inverse_ref, inverse_sem)
    inverse_copy.start()
    for slot in range(2):
        for c in range(8):
            for b in range(4):
                first = c * 16 + b * 4
                rows[first : first + 4] = got_ref[b * 8 + c, slot * 4 : slot * 4 + 4].astype(F32)

        @pl.loop(0, BLK // CHUNK)
        def _(step):
            fetch(slot, step).wait()
            base = pl.multiple_of(step * CHUNK, CHUNK)
            products(
                lambda first: x_ref[slot, pl.ds(base + first, 32)],
                32,
                rows,
                slabs_ref.at[slot],
                acc,
                step,
            )

        done[slot * BLK : (slot + 1) * BLK] = acc[...].astype(BF)
    inverse_copy.wait()
    turned = jnp.dot(done[...], inverse_ref[...], preferred_element_type=F32).astype(BF)
    for slot in range(2):
        for c in range(8):
            for h in range(2):
                first, to = slot * BLK + h * 64 + c * 8, slot * 16 + h * 8
                out_ref[c, to : to + 8] = turned[first : first + 8]


PARAMS = pltpu.CompilerParams(vmem_limit_bytes=51 * 2**20)
COST = pl.CostEstimate(flops=2 * 2 * 128**3 * 1024, bytes_accessed=12 * 2**20, transcendentals=0)


def whole(x):
    return pl.BlockSpec(x.shape, lambda *ids: (0,) * len(x.shape))


def scratch_for(r):
    return [pltpu.VMEM((BLK, r), F32), pltpu.VMEM((BLK, r), F32)]


def first_products(scalars, x, others, slabs):
    r = others[0].shape[-1]
    outs = [jax.ShapeDtypeStruct((32, 8, r), BF), jax.ShapeDtypeStruct((32, 128), F32)]
    return pl.pallas_call(
        first_kernel,
        grid_spec=pltpu.PrefetchScalarGridSpec(
            num_scalar_prefetch=1,
            grid=(2, BLK // CHUNK),
            in_specs=[
                pl.BlockSpec((1, BLK, CHUNK, BLK), lambda s, q, sc: (s, 0, q, 0)),
                *[whole(o) for o in others],
                pl.BlockSpec((1, BLK, r), lambda s, q, sc: (s, 0, 0)),
            ],
            out_specs=[whole(o) for o in outs],
            scratch_shapes=scratch_for(r),
        ),
        out_shape=outs,
        compiler_params=PARAMS,
        cost_estimate=COST,
    )(scalars, x, *others, slabs)


def second_products(x, inverse, others):
    r = inverse.shape[0]
    out = jax.ShapeDtypeStruct((8, 32, r), BF)
    return pl.pallas_call(
        second_kernel,
        grid=(1,),
        in_specs=[
            *[pl.BlockSpec(memory_space=pltpu.HBM)] * 2,
            *[whole(o) for o in others],
        ],
        out_specs=whole(out),
        scratch_shapes=[
            *scratch_for(r),
            pltpu.VMEM((2 * BLK, r), BF),
            pltpu.VMEM(x.shape, BF),
            pltpu.VMEM((r, r), BF),
            pltpu.SemaphoreType.DMA((2, BLK // CHUNK)),
            pltpu.SemaphoreType.DMA(()),
        ],
        out_shape=out,
        compiler_params=PARAMS,
        cost_estimate=COST,
    )(x, inverse, *others)


def choose_kernel(sc, along_ref, *refs):
    *send_refs, rows_ref = refs
    for ref, distance in zip(send_refs, (0, 1, 3, 2)):
        to = lax.rem(lax.axis_index("ja") + distance, 4)
        for s in range(2):
            for g in range(2):
                ref[s * 2 + g] = along_ref[2 * sc[to * 2 + s] + g, 0:16]
    for a in range(8):
        rows_ref[a] = along_ref[a, 16:24]


def chosen_pieces(layers, along):
    r = along.shape[-1]
    outs = [jax.ShapeDtypeStruct((4, 16, r), BF)] * 4 + [jax.ShapeDtypeStruct((8, 8, r), BF)]
    return pl.pallas_call(
        choose_kernel,
        grid_spec=pltpu.PrefetchScalarGridSpec(
            num_scalar_prefetch=1,
            grid=(1,),
            in_specs=[whole(along)],
            out_specs=[whole(o) for o in outs],
        ),
        out_shape=outs,
        compiler_params=pltpu.CompilerParams(vmem_limit_bytes=16 * 2**20),
    )(layers, along)


def body(
    blocks, coordinates, occupancy, second_factor, third_factor, inverse_first, inverse_second
):
    r = inverse_first.shape[0]
    b, c = lax.axis_index("ja"), lax.axis_index("ka")
    own_blocks = blocks.reshape(2, BLK, BLK, BLK)
    places = coordinates.reshape(3, 2)

    mine = jnp.concatenate([third_factor[0], second_factor[0]], axis=0)
    along = lax.all_to_all(
        jnp.broadcast_to(mine, (8, *mine.shape)), "ia", 0, 0, tiled=True
    )
    tags = jnp.concatenate(
        [places.reshape(6), occupancy.reshape(2), jnp.zeros((120,), jnp.int32)]
    ).astype(F32)
    column = jnp.where((jnp.arange(4) == b)[:, None], tags[None, :], 0.0)
    column = column + rotated(column, "ja", 1) + rotated(column, "ja", 2) + rotated(column, "ja", 3)
    along, column = lax.optimization_barrier((along, column))

    layers = column[:, 4:6].reshape(8).astype(jnp.int32)
    *send, row_piece = chosen_pieces(layers, along)
    slabs = [send[0]] + [rotated(send[e], "ja", d) for e, d in ((1, 1), (2, 3), (3, 2))]
    own = [row_piece] + [rotated(row_piece, "ka", d) for d in (2, 6, 4)]
    slabs = layer_slabs(slabs)
    own = jnp.stack(own)
    other = core_swap(own)

    contribution, table = first_products(
        places.reshape(6), own_blocks, (own, other, column), slabs
    )

    arrived = lax.all_to_all(contribution, ("ja", "ka"), 0, 0, tiled=True)
    table = table + core_swap(table)
    table = table + rotated(table, "ka", 2) + rotated(table, "ka", 4) + rotated(table, "ka", 6)
    tag = jnp.repeat(table[:, 0:2].reshape(64), 4)
    weight = jnp.repeat(table[:, 6:8].reshape(64), 4)
    fine = jnp.arange(256) % 4
    owned_block, owned_fine = jnp.arange(16) // 4, jnp.arange(16) % 4
    match = (owned_block[:, None] == tag[None, :]) & (owned_fine[:, None] == fine[None, :])
    pick = jnp.where(match & (weight[None, :] > 0), 1, 0).astype(BF)
    give = jnp.where(match.T, 1, 0).astype(BF)
    owned = jnp.dot(pick, arrived.reshape(256, r), preferred_element_type=F32)
    new_rows = jnp.dot(owned.astype(BF), inverse_first, preferred_element_type=F32).astype(BF)
    sent = jnp.dot(give, new_rows, preferred_element_type=F32).astype(BF).reshape(32, 8, r)
    got = lax.all_to_all(sent, ("ja", "ka"), 0, 0, tiled=True)

    by_block = new_rows.reshape(4, 4, r)
    first_new = jnp.zeros((4, 4, r), BF)
    for d in range(4):
        piece = lax.dynamic_index_in_dim(by_block, (b + d) % 4, 0)
        if d:
            piece = rotated(piece, "ja", d)
        first_new = lax.dynamic_update_slice_in_dim(first_new, piece, (b - d) % 4, 0)
    first_new = first_new.reshape(1, 16, r)

    contribution = second_products(own_blocks, inverse_second, (got, slabs))
    arrived = lax.all_to_all(contribution, "ka", 0, 0, tiled=True)
    mine = lax.dynamic_slice_in_dim(table, b * 8, 8, 0)
    tag = jnp.repeat(mine[:, 2:4].reshape(16), 16)
    weight = jnp.repeat(mine[:, 6:8].reshape(16), 16)
    fine = jnp.arange(256) % 16
    owned_block, owned_fine = jnp.arange(64) // 16, jnp.arange(64) % 16
    match = (owned_block[:, None] == tag[None, :]) & (owned_fine[:, None] == fine[None, :])
    pick = jnp.where(match & (weight[None, :] > 0), 1, 0).astype(BF)
    partial = jnp.dot(pick, arrived.reshape(256, r), preferred_element_type=F32).astype(BF)
    last = lax.all_to_all(partial.reshape(8, 8, r), "ia", 0, 0, tiled=True)
    total = last[0].astype(F32)
    for a in range(1, 8):
        total = total + last[a].astype(F32)
    return first_new, total.astype(BF)[None]


def solution(mesh):
    in_specs = (
        P("ia", "ja", "ka", None, None, None),
        P(None, "ia", "ja", "ka"),
        P("ia", "ja", "ka"),
        P("ja", ("ia", "ka"), None),
        P("ka", ("ia", "ja"), None),
        P(),
        P(),
    )
    out_specs = (P("ia", ("ja", "ka"), None), P("ja", ("ia", "ka"), None))
    return jax.shard_map(body, mesh=mesh, in_specs=in_specs, out_specs=out_specs, check_vma=False)
```

```python
import jax
import jax.numpy as jnp
from jax import lax
from jax.experimental import pallas as pl
from jax.experimental.pallas import tpu as pltpu
from jax.sharding import PartitionSpec as P

BLK = 128
CHUNK = 32
BF = jnp.bfloat16
F32 = jnp.float32


def rotated(x, axis, distance):
    n = lax.axis_size(axis)
    return lax.ppermute(x, axis, [(i, (i + distance) % n) for i in range(n)])


def core_swap(x):
    return lax.ppermute(x, "ka", [(i, i ^ 1) for i in range(lax.axis_size("ka"))])


def products(planes, group, rows, slab, acc, step):
    @pl.when(step == 0)
    def _():
        acc[...] = jnp.zeros_like(acc)

    left = rows[pl.ds(pl.multiple_of(step * CHUNK, CHUNK), CHUNK), :].astype(BF)
    width = acc.shape[-1] // 4
    for first in range(0, CHUNK, group):
        tiles = planes(first)
        lhs = jnp.concatenate([tiles[j] for j in range(group)], axis=1)
        for n in range(4):
            cols = slice(n * width, (n + 1) * width)
            layer = slab[:, cols]
            khatri = jnp.concatenate(
                [layer * left[j : j + 1, cols] for j in range(first, first + group)], axis=0
            )
            acc[:, cols] += jnp.dot(lhs, khatri, preferred_element_type=F32)


def for_slot(slot, when, todo):
    for s in range(2):

        @pl.when((slot == s) & when)
        def _():
            todo(s)


def layers_kernel(l0, l1, l2, l3, out_ref):
    for ref, distance in zip((l0, l1, l2, l3), (0, 1, 3, 2)):
        owner = lax.rem(lax.axis_index("ja") - distance + 4, 4)
        for s in range(2):
            for g in range(2):
                first = pl.multiple_of((g * 4 + owner) * 16, 16)
                out_ref[s, pl.ds(first, 16), :] = ref[s * 2 + g]


def layer_slabs(pieces):
    out = jax.ShapeDtypeStruct((2, BLK, pieces[0].shape[-1]), BF)
    return pl.pallas_call(
        layers_kernel,
        grid=(1,),
        in_specs=[pl.BlockSpec(memory_space=pltpu.VMEM)] * 4,
        out_specs=whole(out),
        out_shape=out,
        compiler_params=PARAMS,
        cost_estimate=pl.CostEstimate(
            flops=2 * 128**3 * 4096, bytes_accessed=2**20, transcendentals=0
        ),
    )(*pieces)


def first_kernel(
    sc, x_ref, own_ref, other_ref, tags_ref, slab_ref, out_ref, table_ref, rows, acc
):
    slot, step = pl.program_id(0), pl.program_id(1)

    @pl.when(step == 0)
    def _():
        col, c = sc[2 + slot], lax.axis_index("ka")
        for e, turn in enumerate((0, 2, 6, 4)):
            mine = lax.rem(c - turn + 8, 8)
            theirs = mine + 1 - 2 * lax.rem(c, 2)
            for h in range(2):
                for ref, owner in ((own_ref, mine), (other_ref, theirs)):
                    first = pl.multiple_of((h * 8 + owner) * 8, 8)
                    rows[pl.ds(first, 8), :] = ref[e, 2 * col + h].astype(F32)

    @pl.when((slot == 0) & (step == 0))
    def _():
        table_ref[...] = jnp.zeros_like(table_ref)
        for b in range(4):
            table_ref[pl.ds(b * 8 + lax.axis_index("ka"), 1), :] = tags_ref[b : b + 1, :]

    def planes(first):
        return jnp.swapaxes(x_ref[0, :, first : first + 16, :], 0, 1)

    products(planes, 16, rows, slab_ref.at[0], acc, step)

    def write(s):
        for b in range(4):
            for c in range(8):
                first = c * 16 + b * 4
                out_ref[b * 8 + c, s * 4 : s * 4 + 4] = acc[first : first + 4].astype(BF)

    for_slot(slot, step == pl.num_programs(1) - 1, write)


def second_kernel(
    x_hbm, inverse_hbm, got_ref, slabs_ref, out_ref, rows, acc, done, *fetched
):
    x_ref, inverse_ref, x_sems, inverse_sem = fetched

    def fetch(slot, step):
        part = pl.ds(pl.multiple_of(step * CHUNK, CHUNK), CHUNK)
        return pltpu.make_async_copy(
            x_hbm.at[slot, part], x_ref.at[slot, part], x_sems.at[slot, step]
        )

    for slot in range(2):
        for step in range(BLK // CHUNK):
            fetch(slot, step).start()
    inverse_copy = pltpu.make_async_copy(inverse_hbm, inverse_ref, inverse_sem)
    inverse_copy.start()
    for slot in range(2):
        for c in range(8):
            for b in range(4):
                first = c * 16 + b * 4
                rows[first : first + 4] = got_ref[b * 8 + c, slot * 4 : slot * 4 + 4].astype(F32)

        @pl.loop(0, BLK // CHUNK)
        def _(step):
            fetch(slot, step).wait()
            base = pl.multiple_of(step * CHUNK, CHUNK)
            products(
                lambda first: x_ref[slot, pl.ds(base + first, 32)],
                32,
                rows,
                slabs_ref.at[slot],
                acc,
                step,
            )

        done[slot * BLK : (slot + 1) * BLK] = acc[...].astype(BF)
    inverse_copy.wait()
    turned = jnp.dot(done[...], inverse_ref[...], preferred_element_type=F32).astype(BF)
    for slot in range(2):
        for c in range(8):
            for h in range(2):
                first, to = slot * BLK + h * 64 + c * 8, slot * 16 + h * 8
                out_ref[c, to : to + 8] = turned[first : first + 8]


PARAMS = pltpu.CompilerParams(vmem_limit_bytes=51 * 2**20)
FIRST_PARAMS = pltpu.CompilerParams(vmem_limit_bytes=46 * 2**20)
COST = pl.CostEstimate(flops=2 * 2 * 128**3 * 1024, bytes_accessed=12 * 2**20, transcendentals=0)


def whole(x):
    return pl.BlockSpec(x.shape, lambda *ids: (0,) * len(x.shape))


def scratch_for(r):
    return [pltpu.VMEM((BLK, r), F32), pltpu.VMEM((BLK, r), F32)]


def first_products(scalars, x, others, slabs):
    r = others[0].shape[-1]
    outs = [jax.ShapeDtypeStruct((32, 8, r), BF), jax.ShapeDtypeStruct((32, 128), F32)]
    return pl.pallas_call(
        first_kernel,
        grid_spec=pltpu.PrefetchScalarGridSpec(
            num_scalar_prefetch=1,
            grid=(2, BLK // CHUNK),
            in_specs=[
                pl.BlockSpec((1, BLK, CHUNK, BLK), lambda s, q, sc: (s, 0, q, 0)),
                *[pl.BlockSpec(memory_space=pltpu.VMEM)] * len(others),
                pl.BlockSpec((1, BLK, r), lambda s, q, sc: (s, 0, 0)),
            ],
            out_specs=[whole(o) for o in outs],
            scratch_shapes=scratch_for(r),
        ),
        out_shape=outs,
        compiler_params=FIRST_PARAMS,
        cost_estimate=COST,
    )(scalars, x, *others, slabs)


def second_products(x, inverse, others):
    r = inverse.shape[0]
    out = jax.ShapeDtypeStruct((8, 32, r), BF)
    return pl.pallas_call(
        second_kernel,
        grid=(1,),
        in_specs=[
            *[pl.BlockSpec(memory_space=pltpu.HBM)] * 2,
            *[pl.BlockSpec(memory_space=pltpu.VMEM)] * len(others),
        ],
        out_specs=whole(out),
        scratch_shapes=[
            *scratch_for(r),
            pltpu.VMEM((2 * BLK, r), BF),
            pltpu.VMEM(x.shape, BF),
            pltpu.VMEM((r, r), BF),
            pltpu.SemaphoreType.DMA((2, BLK // CHUNK)),
            pltpu.SemaphoreType.DMA(()),
        ],
        out_shape=out,
        compiler_params=PARAMS,
        cost_estimate=COST,
    )(x, inverse, *others)


def choose_kernel(sc, along_ref, *refs):
    *send_refs, rows_ref = refs
    for ref, distance in zip(send_refs, (0, 1, 3, 2)):
        to = lax.rem(lax.axis_index("ja") + distance, 4)
        for s in range(2):
            for g in range(2):
                ref[s * 2 + g] = along_ref[2 * sc[to * 2 + s] + g, 0:16]
    for a in range(8):
        rows_ref[a] = along_ref[a, 16:24]


def chosen_pieces(layers, along):
    r = along.shape[-1]
    outs = [jax.ShapeDtypeStruct((4, 16, r), BF)] * 4 + [jax.ShapeDtypeStruct((8, 8, r), BF)]
    return pl.pallas_call(
        choose_kernel,
        grid_spec=pltpu.PrefetchScalarGridSpec(
            num_scalar_prefetch=1,
            grid=(1,),
            in_specs=[whole(along)],
            out_specs=[whole(o) for o in outs],
        ),
        out_shape=outs,
        compiler_params=pltpu.CompilerParams(vmem_limit_bytes=16 * 2**20),
    )(layers, along)


def body(
    blocks, coordinates, occupancy, second_factor, third_factor, inverse_first, inverse_second
):
    r = inverse_first.shape[0]
    b, c = lax.axis_index("ja"), lax.axis_index("ka")
    own_blocks = blocks.reshape(2, BLK, BLK, BLK)
    places = coordinates.reshape(3, 2)

    mine = jnp.concatenate([third_factor[0], second_factor[0]], axis=0)
    along = lax.all_to_all(
        jnp.broadcast_to(mine, (8, *mine.shape)), "ia", 0, 0, tiled=True
    )
    tags = jnp.concatenate(
        [places.reshape(6), occupancy.reshape(2), jnp.zeros((120,), jnp.int32)]
    ).astype(F32)
    column = jnp.where((jnp.arange(4) == b)[:, None], tags[None, :], 0.0)
    column = column + rotated(column, "ja", 1) + rotated(column, "ja", 2) + rotated(column, "ja", 3)
    along, column = lax.optimization_barrier((along, column))

    layers = column[:, 4:6].reshape(8).astype(jnp.int32)
    *send, row_piece = chosen_pieces(layers, along)
    slabs = [send[0]] + [rotated(send[e], "ja", d) for e, d in ((1, 1), (2, 3), (3, 2))]
    own = [row_piece] + [rotated(row_piece, "ka", d) for d in (2, 6, 4)]
    slabs = layer_slabs(slabs)
    own = jnp.stack(own)
    other = core_swap(own)

    contribution, table = first_products(
        places.reshape(6), own_blocks, (own, other, column), slabs
    )

    arrived = lax.all_to_all(contribution, ("ja", "ka"), 0, 0, tiled=True)
    table = table + core_swap(table)
    table = table + rotated(table, "ka", 2) + rotated(table, "ka", 4) + rotated(table, "ka", 6)
    tag = jnp.repeat(table[:, 0:2].reshape(64), 4)
    weight = jnp.repeat(table[:, 6:8].reshape(64), 4)
    fine = jnp.arange(256) % 4
    owned_block, owned_fine = jnp.arange(16) // 4, jnp.arange(16) % 4
    match = (owned_block[:, None] == tag[None, :]) & (owned_fine[:, None] == fine[None, :])
    pick = jnp.where(match & (weight[None, :] > 0), 1, 0).astype(BF)
    give = jnp.where(match.T, 1, 0).astype(BF)
    owned = jnp.dot(pick, arrived.reshape(256, r), preferred_element_type=F32)
    new_rows = jnp.dot(owned.astype(BF), inverse_first, preferred_element_type=F32).astype(BF)
    sent = jnp.dot(give, new_rows, preferred_element_type=F32).astype(BF).reshape(32, 8, r)
    got = lax.all_to_all(sent, ("ja", "ka"), 0, 0, tiled=True)

    by_block = new_rows.reshape(4, 4, r)
    first_new = jnp.zeros((4, 4, r), BF)
    for d in range(4):
        piece = lax.dynamic_index_in_dim(by_block, (b + d) % 4, 0)
        if d:
            piece = rotated(piece, "ja", d)
        first_new = lax.dynamic_update_slice_in_dim(first_new, piece, (b - d) % 4, 0)
    first_new = first_new.reshape(1, 16, r)

    contribution = second_products(own_blocks, inverse_second, (got, slabs))
    arrived = lax.all_to_all(contribution, "ka", 0, 0, tiled=True)
    mine = lax.dynamic_slice_in_dim(table, b * 8, 8, 0)
    tag = jnp.repeat(mine[:, 2:4].reshape(16), 16)
    weight = jnp.repeat(mine[:, 6:8].reshape(16), 16)
    fine = jnp.arange(256) % 16
    owned_block, owned_fine = jnp.arange(64) // 16, jnp.arange(64) % 16
    match = (owned_block[:, None] == tag[None, :]) & (owned_fine[:, None] == fine[None, :])
    pick = jnp.where(match & (weight[None, :] > 0), 1, 0).astype(BF)
    partial = jnp.dot(pick, arrived.reshape(256, r), preferred_element_type=F32).astype(BF)
    last = lax.all_to_all(partial.reshape(8, 8, r), "ia", 0, 0, tiled=True)
    total = last[0].astype(F32)
    for a in range(1, 8):
        total = total + last[a].astype(F32)
    return first_new, total.astype(BF)[None]


def solution(mesh):
    in_specs = (
        P("ia", "ja", "ka", None, None, None),
        P(None, "ia", "ja", "ka"),
        P("ia", "ja", "ka"),
        P("ja", ("ia", "ka"), None),
        P("ka", ("ia", "ja"), None),
        P(),
        P(),
    )
    out_specs = (P("ia", ("ja", "ka"), None), P("ja", ("ia", "ka"), None))
    return jax.shard_map(body, mesh=mesh, in_specs=in_specs, out_specs=out_specs, check_vma=False)
```
